512 devices in a mesh: brick: 64 (over y_hi, z, core), chan: 8 (over y_lo, x).
Axes of the slice: x: 4, y: 8 (y_hi: 4, y_lo: 2; y = y_hi * 2 + y_lo), z: 8, core: 2. Of those that a mesh axis runs over, the one named last changes fastest.
Arguments:
- features: bfloat16 [512, 32768], P('chan', 'brick'), may hold values from -6 to 6
- positions: float32 [3, 32768], P(None, 'brick'), may hold values from 0 to 1, as said below
- lists: int32 [256, 4], P('brick'), may hold values from 0 to 7, as said below
- counts: int32 [256], P('brick'), may hold values from 1 to 4, as said below
- fourier_filter: float32 [512, 4096], P('chan'), may hold values from 0.5 to 4
- radial_weights: float32 [8, 512], P(None, 'chan'), may hold values from -4 to 4
- norm_gain: float32 [512], replicated, may hold values from 0.1 to 1.9
- mlp_in: bfloat16 [1024, 512], P(None, 'chan'), may hold values from -0.25 to 0.25
- mlp_out: bfloat16 [512, 1024], P('chan'), may hold values from -0.1875 to 0.1875
Outputs:
- updated: bfloat16 [512, 32768], P(None, ('brick', 'chan'))
The draws below stay inside these ranges and needn't reach their ends.
Inputs may be any that keep to these rules, and one draw needn't show every extreme that they name: Row g of lists holds 4 different values from (g mod 4) to (g mod 4) + 4. `counts`: the value 4 occurs in every draw. `positions`: for an atom of block j of its brick (j = its index // 128 mod 4) the first coordinate lies between j / 4 and (j + 1) / 4; the other two lie in [0, 1).
All inputs are finite; a program needn't handle non-finite values.
Results may differ from the reference program's by a relative error of at most 0.0055.
The reference program's roundings to bfloat16 on the way count: a program that leaves them out, or rounds other values in their place, can miss the bound.
Values may be sent and summed in bfloat16 or wider, within the bound.
A program may use at most 64 MiB of HBM per device.

```python
import math
import jax
import jax.numpy as jnp
from jax import lax

C = 512
KSIDE = 16
NK = 4096
HID = 1024
NBASIS = 8
BLOCK = 128
BLK_DEV = 4
REACH = 2
LIST = 4
A_DEV = 512
ATOMS = 32768
NBLOCKS = 256
N_BRICK = 64


def draw_positions(key, part):
    first_key = jax.random.fold_in(key, 31)
    second_key = jax.random.fold_in(key, 32)
    fraction = jax.random.uniform(first_key, (ATOMS,), jnp.float32, 0.0, 0.999)
    block_local = (jnp.arange(ATOMS, dtype=jnp.int32) // BLOCK % BLK_DEV).astype(jnp.float32)
    along_first = (block_local + fraction) / BLK_DEV
    across = jax.random.uniform(second_key, (2, ATOMS), jnp.float32, 0.0, 0.999)
    return jnp.concatenate([along_first[None, :], across], axis=0)


def draw_lists(key, part):
    window = 2 * REACH + 1
    scores = jax.random.randint(jax.random.fold_in(key, 11), (NBLOCKS, window), 0, 1 << 20) * window
    scores = scores + jnp.arange(window, dtype=jnp.int32)[None, :]
    ordering = jnp.argsort(scores, axis=1, stable=True).astype(jnp.int32)
    local_block = (jnp.arange(NBLOCKS, dtype=jnp.int32) % BLK_DEV)[:, None]
    return (local_block + ordering[:, :LIST]).astype(jnp.int32)


def draw_counts(key, part):
    brick_total = NBLOCKS // BLK_DEV
    brick_loads = jax.random.randint(jax.random.fold_in(key, 21), (brick_total,), 1, LIST + 1)
    busiest = jax.random.randint(jax.random.fold_in(key, 22), (), 0, brick_total)
    brick_loads = jnp.where(jnp.arange(brick_total, dtype=jnp.int32) == busiest, LIST, brick_loads)
    block_rows = jnp.arange(NBLOCKS, dtype=jnp.int32)
    lowered = brick_loads[block_rows // BLK_DEV] - jax.random.randint(jax.random.fold_in(key, 23), (NBLOCKS,), 0, 2)
    clipped = jnp.clip(lowered, 1, LIST)
    return jnp.where(block_rows == busiest * BLK_DEV, LIST, clipped).astype(jnp.int32)


def block_scale(stream_key, dims, split, least, top_value):
    loudness, own = 1.0, jax.random.fold_in(stream_key, 6)
    for axis_at, blocks in split:
        steps = jnp.exp(jax.random.uniform(jax.random.fold_in(own, axis_at), (blocks,), jnp.float32, least / len(split), top_value / len(split)))
        loudness = loudness * jnp.repeat(steps, dims[axis_at] // blocks).reshape([-1 if axis == axis_at else 1 for axis in range(len(dims))])
    return loudness


def centred(key, extent, width, reach, split=(), kind=jnp.bfloat16):
    drawn = jax.random.normal(key, extent, jnp.float32) * width
    if len(split) > 0:
        drawn = block_scale(key, extent, split, -0.22, 0.18) * drawn
    return jnp.clip(drawn, min=-reach, max=reach).astype(kind)


def setup_inputs(seed: int = 0) -> dict:
    key_list = jax.random.split(jax.random.key(seed), 10)
    features = centred(key_list[0], (C, ATOMS), 1.0, 6.0, ((0, 8), (1, 64)))
    positions = draw_positions(jax.random.fold_in(key_list[9], 71), 0)
    lists = draw_lists(jax.random.fold_in(key_list[9], 71), 0)
    counts = draw_counts(jax.random.fold_in(key_list[9], 71), 0)
    fourier_filter = jnp.clip(jnp.exp(math.log(4.0) - 2.0794415 * jax.random.uniform(key_list[4], (C, NK), jnp.float32) ** block_scale(key_list[4], (C, NK), ((0, 8),), -0.2, 0.2)), 0.5, 4.0)
    radial_weights = centred(key_list[5], (NBASIS, C), 0.3, 4.0, ((1, 8),), jnp.float32)
    norm_gain = jnp.clip(1.0 + 0.18 * jax.random.normal(key_list[6], (C,), jnp.float32), 0.1, 1.9)
    mlp_in = centred(key_list[7], (HID, C), C ** -0.5, 0.25, ((1, 8),))
    mlp_out = centred(key_list[8], (C, HID), HID ** -0.5, 0.1875, ((0, 8),))
    return {"features": features, "positions": positions, "lists": lists, "counts": counts, "fourier_filter": fourier_filter, "radial_weights": radial_weights, "norm_gain": norm_gain, "mlp_in": mlp_in, "mlp_out": mlp_out}


brick_width = 4.0
cross_width = 8.0
cutoff = 2.0
epsilon = 1e-06

def wave_table(side_count, brick_count):
    wave_index = jnp.arange(side_count ** 3, dtype=jnp.int32)
    first_number = (wave_index % side_count + 1).astype(jnp.float32)
    second_number = (wave_index // side_count % side_count - side_count // 2).astype(jnp.float32)
    third_number = (wave_index // (side_count * side_count) - side_count // 2).astype(jnp.float32)
    along_x = first_number * (2.0 * math.pi / (brick_count * brick_width))
    along_y = second_number * (2.0 * math.pi / cross_width)
    along_z = third_number * (2.0 * math.pi / cross_width)
    return (along_x, along_y, along_z)

def angle_rows(places, brick_float, along_x, along_y, along_z):
    x_place = (brick_float + places[0]) * brick_width
    y_place = places[1] * cross_width
    z_place = places[2] * cross_width
    return x_place[:, None] * along_x[None, :] + y_place[:, None] * along_y[None, :] + z_place[:, None] * along_z[None, :]

def phase_rows(places, brick_float, wave_vectors):
    angles = angle_rows(places, brick_float, wave_vectors[0], wave_vectors[1], wave_vectors[2])
    return jnp.concatenate([jnp.cos(angles), jnp.sin(angles)], axis=1).astype(jnp.bfloat16)

def radial_basis(delta_x, delta_y, delta_z, basis_count):
    squared = delta_x * delta_x + delta_y * delta_y + delta_z * delta_z
    distance = jnp.sqrt(squared)
    envelope = jnp.square(jnp.maximum(1.0 - squared / (cutoff * cutoff), 0.0))
    spacing = cutoff / (basis_count - 1)
    centres = (jnp.arange(basis_count, dtype=jnp.float32) * spacing).reshape((basis_count,) + (1,) * distance.ndim)
    scaled_gap = (distance[None] - centres) / spacing
    return (jnp.exp(-scaled_gap * scaled_gap) * envelope[None]).astype(jnp.bfloat16)

def reference(features, positions, lists, counts, fourier_filter, radial_weights, norm_gain, mlp_in, mlp_out):
    wave_vectors = wave_table(KSIDE, N_BRICK)
    inverse = 1.0 / math.sqrt(ATOMS)
    feature_bricks = jnp.transpose(features.reshape(C, N_BRICK, A_DEV), (1, 0, 2))
    place_bricks = jnp.transpose(positions.reshape(3, N_BRICK, A_DEV), (1, 0, 2))
    brick_ids = jnp.arange(N_BRICK, dtype=jnp.int32)

    def add_brick(partial_value, bundle):
        brick_id, feature_rows, places = bundle
        phases = phase_rows(places, brick_id.astype(jnp.float32), wave_vectors)
        return (partial_value + jnp.dot(feature_rows, phases, preferred_element_type=jnp.float32), None)
    partial_value, unused = lax.scan(add_brick, jnp.zeros((C, 2 * NK), jnp.float32), (brick_ids, feature_bricks, place_bricks))
    filtered = (jnp.concatenate([fourier_filter, fourier_filter], axis=1) * (partial_value * inverse)).astype(jnp.bfloat16)

    def evaluate(bundle):
        brick_id, places = bundle
        phases = phase_rows(places, brick_id.astype(jnp.float32), wave_vectors)
        return lax.dot_general(filtered, phases, (((1,), (1,)), ((), ())), preferred_element_type=jnp.float32) * inverse
    ewald = lax.map(evaluate, (brick_ids, place_bricks))
    ewald = jnp.transpose(ewald, (1, 0, 2)).reshape(C, ATOMS)
    feature_blocks = features.reshape(C, NBLOCKS, BLOCK)
    place_blocks = positions.reshape(3, NBLOCKS, BLOCK)

    def one_target(target):
        brick_id = target // BLK_DEV
        relative = lists[target] - REACH
        global_block = ((brick_id * BLK_DEV + relative) % NBLOCKS).astype(jnp.int32)
        offsets = (relative // BLK_DEV).astype(jnp.float32)
        source_places = jnp.take(place_blocks, global_block, axis=1)
        target_places = lax.dynamic_index_in_dim(place_blocks, target, 1, keepdims=False)
        source_x = source_places[0] + offsets[:, None]
        delta_x = (source_x[:, :, None] - target_places[0][None, None, :]) * brick_width
        delta_y = (source_places[1][:, :, None] - target_places[1][None, None, :]) * cross_width
        delta_z = (source_places[2][:, :, None] - target_places[2][None, None, :]) * cross_width
        radial_terms = radial_basis(delta_x, delta_y, delta_z, NBASIS)
        source_features = jnp.take(feature_blocks, global_block, axis=1)
        scaled = (source_features[:, :, None, :].astype(jnp.float32) * radial_weights.T[:, None, :, None]).astype(jnp.bfloat16)
        mask_weight = (jnp.arange(LIST, dtype=jnp.int32) < counts[target]).astype(jnp.float32)
        return jnp.einsum('clmb,mlba,l->ca', scaled.astype(jnp.float32), radial_terms.astype(jnp.float32), mask_weight)
    messages = lax.map(one_target, jnp.arange(NBLOCKS, dtype=jnp.int32))
    messages = jnp.transpose(messages, (1, 0, 2)).reshape(C, ATOMS)
    mixed = (features.astype(jnp.float32) + messages + ewald).astype(jnp.bfloat16)
    values = mixed.astype(jnp.float32)
    mean_square = lax.optimization_barrier(jnp.mean(values * values, axis=0, keepdims=True))
    normed = (values * lax.rsqrt(mean_square + epsilon) * norm_gain[:, None]).astype(jnp.bfloat16)
    hidden = jnp.dot(mlp_in, normed, preferred_element_type=jnp.float32)
    active = jax.nn.gelu(hidden).astype(jnp.bfloat16)
    return (values + jnp.dot(mlp_out, active, preferred_element_type=jnp.float32)).astype(jnp.bfloat16)
```

```python
import math

import jax
import jax.numpy as jnp
from jax import lax
from jax.experimental import pallas as pl
from jax.experimental.pallas import tpu as pltpu
from jax.sharding import PartitionSpec as P

MESH = pl.DeviceIdType.MESH
F32 = jnp.float32
BF16 = jnp.bfloat16

NZ = 8
NY = 4
NX = 4
NBRICK = NZ * NY * 2
NCHAN = 8
CD = 64
AD = 512
C = 512
HID = 1024
NB = 8
KS = 16
WIDTH, CROSS, CUTOFF, EPS = 4.0, 8.0, 2.0, 1e-06
SPACING = CUTOFF / (NB - 1)
INVERSE = 1.0 / math.sqrt(AD * NBRICK)

NN = (((1,), (0,)), ((), ()))
NT = (((1,), (1,)), ((), ()))


def dot(a, b, dims):
    return lax.dot_general(a, b, dims, preferred_element_type=F32)


def turn(u):
    u = u - jnp.floor(u + 0.5)
    th = u * math.pi
    q = th * th
    s = -1.0 / 39916800
    for n in (362880, -5040, 120, -6, 1):
        s = s * q + 1.0 / n
    s = s * th
    c = 1.0 / 479001600
    for n in (-3628800, 40320, -720, 24, -2, 1):
        c = c * q + 1.0 / n
    return 1.0 - 2.0 * s * s, 2.0 * s * c


def kernel(
    feat, pos, lists, counts, filt, rw, gain, win, wout, out,
    ph, trig, cxy, part, sib, ss, rs1, t2, rs2, fg, fq, flt,
    fe, pe, pt, sc, bas, msg, ew, wg, ms, mr,
    local_sem, halo_s, halo_r, core_s, core_r, rs1_s, rs1_r, rs2_s, rs2_r,
    ag1_s, ag1_r, ag2_s, ag2_r, fw_s, fw_r, w_s, w_r, wf_s, wf_r, a2a_s, a2a_r,
):
    brick = lax.axis_index("brick")
    chan = lax.axis_index("chan")
    core = lax.rem(brick, 2)
    z = lax.rem(brick // 2, NZ)
    y = brick // (2 * NZ)
    x = lax.rem(chan, NX)
    ylo = chan // NX
    first = core == 0
    second = core == 1

    def at(yy, zz, cc):
        return ((lax.rem(yy, NY) * NZ + lax.rem(zz, NZ)) * 2 + cc, chan)

    sibling = at(y, z, 1 - core)
    left = (lax.rem(brick + NBRICK - 1, NBRICK), chan)
    right = (lax.rem(brick + 1, NBRICK), chan)
    z_peer = lambda d: at(y, z + d, core)
    y_peer = lambda d: at(y + d, z, core)
    chan_peer = lambda d: (brick, lax.rem(chan + d, NCHAN))
    x_peer = lambda d: (brick, ylo * NX + lax.rem(x + d, NX))
    ylo_peer = (brick, (1 - ylo) * NX + x)

    barrier = pltpu.get_barrier_semaphore()
    partners = [z_peer(d) for d in range(1, NZ)] + [y_peer(d) for d in range(1, NY)]
    partners += [chan_peer(d) for d in range(1, NCHAN)] + [left, right]
    for device in partners:
        pl.semaphore_signal(barrier, inc=1, device_id=device, device_id_type=MESH)

    eye = (
        lax.broadcasted_iota(jnp.int32, (CD, CD), 0)
        == lax.broadcasted_iota(jnp.int32, (CD, CD), 1)
    ).astype(BF16)
    own = jnp.where(first, core * 32 + z * NY + y, y * NZ + z)
    filter_copy = pltpu.make_async_copy(
        filt.at[:, pl.ds(pl.multiple_of(own * 128, 128), 128)], flt, local_sem
    )
    filter_copy.start()
    win_t = dot(eye, win[...], NT).astype(BF16)
    wg[core, chan] = jnp.where(first, win_t, wout[...])
    fe[1] = feat[:, 0:256]
    fe[2] = feat[:, 256:512]
    for half in range(2):
        pe[1 + half] = jnp.zeros((8, 256), F32)
        pe[1 + half, 0:3, :] = pos[:, half * 256 : (half + 1) * 256]

    pl.semaphore_wait(barrier, len(partners))

    def remote(src, dst, send, recv, device):
        return pltpu.make_async_remote_copy(
            src_ref=src, dst_ref=dst, send_sem=send, recv_sem=recv,
            device_id=device, device_id_type=MESH,
        )

    halos = [
        remote(fe.at[1], fe.at[3], halo_s.at[0], halo_r.at[0], left),
        remote(fe.at[2], fe.at[0], halo_s.at[1], halo_r.at[1], right),
        remote(pe.at[1], pe.at[3], halo_s.at[2], halo_r.at[2], left),
        remote(pe.at[2], pe.at[0], halo_s.at[3], halo_r.at[3], right),
    ]
    for copy in halos:
        copy.start()

    mine = wg.at[core, chan]
    weight_y = remote(mine, mine, w_s.at[0], w_r.at[0], ylo_peer)
    weight_y.start()
    weight_x = [remote(mine, mine, w_s.at[d], w_r.at[d], x_peer(d)) for d in range(1, NX)]
    for copy in weight_x:
        copy.start()

    px, py, pz = pos[0:1, :], pos[1:2, :], pos[2:3, :]
    number = lax.broadcasted_iota(jnp.int32, (KS, 1), 0).astype(F32)
    xturn = (brick.astype(F32) + px) * (1.0 / NBRICK)
    cx, sx = turn((number + 1.0) * xturn)
    cy, sy = turn((number - KS // 2) * py)
    cz, sz = turn((number - KS // 2) * pz)
    trig[0], trig[1] = cz, sz
    for r in range(KS):
        rows = slice(r * KS, (r + 1) * KS)
        cxy[0, rows, :] = cx * cy[r : r + 1, :] - sx * sy[r : r + 1, :]
        cxy[1, rows, :] = sx * cy[r : r + 1, :] + cx * sy[r : r + 1, :]

    features = feat[...]

    def core_copy(i):
        return remote(part.at[i, 1 - core], sib.at[i], core_s.at[i], core_r.at[i], sibling)

    def compute(i):
        za = lax.rem(z + i + 1, NZ)
        yb = lax.rem(y + i // 2 + 1, NY)
        for half in range(2):
            na = 2 * za + half
            nb = 4 * yb + 2 * lax.rem(i, 2) + half
            ca, sa = trig[0, pl.ds(na, 1), :], trig[1, pl.ds(na, 1), :]
            cb, sb = trig[0, pl.ds(nb, 1), :], trig[1, pl.ds(nb, 1), :]
            for g in range(8):
                rows = slice(g * 32, (g + 1) * 32)
                cc, cs = cxy[0, rows, :], cxy[1, rows, :]
                ph[0, na, rows, :] = (cc * ca - cs * sa).astype(BF16)
                ph[1, nb, rows, :] = (cs * cb + cc * sb).astype(BF16)
            cols = slice(half * 256, (half + 1) * 256)
            part[i, 0, :, cols] = dot(features, ph[0, na], NT)
            part[i, 1, :, cols] = dot(features, ph[1, nb], NT)
        core_copy(i).start()

    def rs1_copy(i):
        device = (
            jnp.where(first, at(y, z + i + 1, 0)[0], at(y + i // 2 + 1, z, 1)[0]),
            chan,
        )
        return remote(ss.at[i], rs1.at[i], rs1_s.at[i], rs1_r.at[i], device)

    def finish(i):
        core_copy(i).wait_recv()
        ss[i] = (part[i, core] + sib[i]).astype(BF16)

        @pl.when(i < 7 - core)
        def _():
            rs1_copy(i).start()

    compute(0)

    def step(i, carry):
        compute(i)
        finish(i - 1)
        return carry

    lax.fori_loop(1, NZ, step, 0)
    finish(NZ - 1)

    weight_y.wait_recv()
    theirs = wg.at[core, (1 - ylo) * NX + x]
    weight_r = [
        remote(theirs, theirs, w_s.at[NX + d], w_r.at[NX + d], x_peer(d)) for d in range(1, NX)
    ]
    for copy in weight_r:
        copy.start()

    for copy in halos:
        copy.wait_recv()
    rw_pad = jnp.concatenate([rw[...], jnp.zeros((NB, CD), F32)], axis=1)
    rw_t = jnp.transpose(rw_pad)[0:CD, :]
    for e in range(8):
        lanes = slice((e % 2) * 128, (e % 2 + 1) * 128)
        shift = -1.0 if e < 2 else (1.0 if e >= 6 else 0.0)
        rows = pe[e // 2, :, lanes]
        at_x = lax.broadcasted_iota(jnp.int32, (8, 128), 0) == 0
        pt[e] = jnp.transpose(jnp.where(at_x, rows + shift, rows))
        block = fe[e // 2, :, lanes].astype(F32)
        for m in range(NB):
            sc[e, :, m * 128 : (m + 1) * 128] = (block * rw_t[:, m : m + 1]).astype(BF16)

    def pair(t, l):
        e = lists[t, l]
        used = jnp.where(l < counts[t], 1.0, 0.0).astype(F32)
        source = pt[e]
        half = t // 2
        lane = pl.ds(pl.multiple_of(lax.rem(t, 2) * 128, 128), 128)
        target = pe[1 + half, :, lane]
        dx = (source[:, 0:1] - target[0:1, :]) * WIDTH
        dy = (source[:, 1:2] - target[1:2, :]) * CROSS
        dz = (source[:, 2:3] - target[2:3, :]) * CROSS
        r2 = dx * dx + dy * dy + dz * dz
        env = jnp.maximum(1.0 - r2 * (1.0 / (CUTOFF * CUTOFF)), 0.0)
        tt = jnp.minimum(jnp.sqrt(r2) * (1.0 / SPACING), float(NB - 1))
        value = jnp.exp(-tt * tt) * (env * env * used)
        ratio = jnp.exp(2.0 * tt)
        bas[0:128, :] = value.astype(BF16)
        for m in range(1, NB):
            value = value * (ratio * math.exp(-(2 * m - 1)))
            bas[m * 128 : (m + 1) * 128, :] = value.astype(BF16)
        return dot(sc[e], bas[...], NN)

    def target_block(t, carry):
        total = lax.fori_loop(
            0, 4, lambda l, acc: acc + pair(t, l), jnp.zeros((CD, 128), F32)
        )
        msg[t] = total
        return carry

    lax.fori_loop(0, 4, target_block, 0)

    def rs2_copy(d):
        slot = jnp.where(first, lax.rem(y + d, NY), lax.rem(z + d, NZ))
        device = (jnp.where(first, at(y + d, z, 0)[0], at(y, z + d, 1)[0]), chan)
        return remote(t2.at[slot], rs2.at[d], rs2_s.at[d], rs2_r.at[d], device)

    ag_a = fg.at[0, pl.ds(z * NY, NY)]
    ag_b = fg.at[1, pl.ds(y * NZ, NZ)]

    @pl.when(first)
    def _():
        for i in range(NZ - 1):
            rs1_copy(i).wait_recv()
        total = ss[NZ - 1].astype(F32)
        for i in range(NZ - 1):
            total = total + rs1[i].astype(F32)
        for k in range(NY):
            t2[k] = total[:, k * 128 : (k + 1) * 128].astype(BF16)
        for d in range(1, NY):
            rs2_copy(d).start()
        for d in range(1, NY):
            rs2_copy(d).wait_recv()
        total = t2[y].astype(F32)
        for d in range(1, NY):
            total = total + rs2[d].astype(F32)
        fq[...] = total

    @pl.when(second)
    def _():
        for i in range(NZ - 2):
            rs1_copy(i).wait_recv()
        for half in range(2):
            total = ss[NZ - 2 + half].astype(F32)
            for i in range(NY - 1):
                total = total + rs1[2 * i + half].astype(F32)
            for k in range(4):
                t2[4 * half + k] = total[:, k * 128 : (k + 1) * 128].astype(BF16)
        for d in range(1, NZ):
            rs2_copy(d).start()
        for d in range(1, NZ):
            rs2_copy(d).wait_recv()
        total = t2[z].astype(F32)
        for d in range(1, NZ):
            total = total + rs2[d].astype(F32)
        fq[...] = total

    filter_copy.wait()
    fg[core, own] = (flt[...] * (fq[...] * INVERSE)).astype(BF16)

    def ag1_copy(d):
        block = fg.at[core, own]
        device = (jnp.where(first, at(y + d, z, 0)[0], at(y, z + d, 1)[0]), chan)
        return remote(block, block, ag1_s.at[d], ag1_r.at[d], device)

    def forward_copy(kind, group, slot):
        size = NY if kind == 0 else NZ
        block = fg.at[kind, pl.ds(group * size, size)]
        return remote(block, block, fw_s.at[slot], fw_r.at[slot], sibling)

    weights_on = remote(wg.at[core], wg.at[core], wf_s, wf_r, sibling)

    def weights_forward():
        for copy in weight_x + weight_r:
            copy.wait_recv()
        weights_on.start()

    def evaluate(kind, group):
        if kind == 0:
            blocks = [fg[0, group * NY + k] for k in range(NY)]
            phase = ph[0, pl.ds(2 * group, 2)].reshape(2 * 256, AD)
        else:
            blocks = [fg[1, group * NZ + k] for k in range(NZ)]
            phase = ph[1, pl.ds(4 * group, 4)].reshape(4 * 256, AD)
        ew[...] += dot(jnp.concatenate(blocks, axis=1), phase, NN)

    ew[...] = jnp.zeros((CD, AD), F32)

    def gather_and_evaluate(kind):
        near = NY if kind == 0 else NZ
        far = NZ if kind == 0 else NY
        here = z if kind == 0 else y
        block = ag_a if kind == 0 else ag_b
        other = 1 - kind
        far_here = y if kind == 0 else z
        for d in range(1, near):
            ag1_copy(d).start()
        weights_forward()
        for d in range(1, near):
            ag1_copy(d).wait_recv()
        peer = z_peer if kind == 0 else y_peer
        copies = [
            remote(block, block, ag2_s.at[d], ag2_r.at[d], peer(d)) for d in range(1, far)
        ]
        for copy in copies:
            copy.start()
        forward_copy(kind, here, 0).start()
        evaluate(kind, here)
        turns = far // (NZ + NY - far) if far > NY else 1
        given = 1 if far > NY else 2
        done = 0
        mine_back = y if kind == 0 else z
        for d in range(far):
            if d:
                copies[d - 1].wait_recv()
                group = lax.rem(here + far - d, far)
                forward_copy(kind, group, d).start()
                evaluate(kind, group)
            if (d + 1) % turns == 0:
                for _ in range(given):
                    group = lax.rem(mine_back + near - done, near)
                    forward_copy(other, group, done).wait_recv()
                    evaluate(other, group)
                    done += 1
        for copy in copies:
            copy.wait_send()
        for d in range(far):
            forward_copy(kind, here, d).wait_send()
        for d in range(1, near):
            ag1_copy(d).wait_send()
            rs2_copy(d).wait_send()

    @pl.when(first)
    def _():
        gather_and_evaluate(0)

    @pl.when(second)
    def _():
        gather_and_evaluate(1)

    for t in range(4):
        lanes = slice(t * 128, (t + 1) * 128)
        mixed = (
            features[:, lanes].astype(F32) + msg[t] + ew[:, lanes] * INVERSE
        ).astype(BF16)
        ms[2 * t] = mixed[:, 0:64]
        ms[2 * t + 1] = mixed[:, 64:128]
    exchange = []
    for d in range(1, NCHAN):
        device = chan_peer(d)
        exchange.append(
            remote(ms.at[device[1]], mr.at[chan], a2a_s.at[d], a2a_r.at[d], device)
        )
        exchange[-1].start()
    mr[chan] = ms[chan]
    remote(wg.at[1 - core], wg.at[1 - core], wf_s, wf_r, sibling).wait_recv()
    for copy in exchange:
        copy.wait_recv()

    values = mr[...].reshape(C, 64)
    values_t = dot(eye, values, NT)
    mean_square = jnp.sum(values_t * values_t, axis=1, keepdims=True) * (1.0 / C)
    normed = (values_t * lax.rsqrt(mean_square + EPS) * gain[...]).astype(BF16)
    hidden = dot(normed, wg[0].reshape(C, HID), NN)
    active = jax.nn.gelu(hidden).astype(BF16)
    mixed_out = dot(wg[1].reshape(C, HID), active, NT)
    out[...] = (values.astype(F32) + mixed_out).astype(BF16)

    for copy in halos + weight_x + weight_r + [weight_y, weights_on] + exchange:
        copy.wait_send()

    def sent(i, carry):
        core_copy(i).wait_send()

        @pl.when(i < 7 - core)
        def _():
            rs1_copy(i).wait_send()

        return carry

    lax.fori_loop(0, NZ, sent, 0)


def body(features, positions, lists, counts, fourier_filter, radial_weights, norm_gain, mlp_in, mlp_out):
    vmem = pl.BlockSpec(memory_space=pltpu.VMEM)
    smem = pl.BlockSpec(memory_space=pltpu.SMEM)
    dma = pltpu.SemaphoreType.DMA
    scratch = [
        pltpu.VMEM((2, KS, 256, AD), BF16),
        pltpu.VMEM((2, KS, AD), F32),
        pltpu.VMEM((2, 256, AD), F32),
        pltpu.VMEM((NZ, 2, CD, 512), F32),
        pltpu.VMEM((NZ, CD, 512), F32),
        pltpu.VMEM((NZ, CD, 512), BF16),
        pltpu.VMEM((NZ, CD, 512), BF16),
        pltpu.VMEM((NZ, CD, 128), BF16),
        pltpu.VMEM((NZ, CD, 128), BF16),
        pltpu.VMEM((2, 32, CD, 128), BF16),
        pltpu.VMEM((CD, 128), F32),
        pltpu.VMEM((CD, 128), F32),
        pltpu.VMEM((4, CD, 256), BF16),
        pltpu.VMEM((4, 8, 256), F32),
        pltpu.VMEM((8, 128, 8), F32),
        pltpu.VMEM((8, CD, NB * 128), BF16),
        pltpu.VMEM((NB * 128, 128), BF16),
        pltpu.VMEM((4, CD, 128), F32),
        pltpu.VMEM((CD, AD), F32),
        pltpu.VMEM((2, NCHAN, CD, HID), BF16),
        pltpu.VMEM((NCHAN, CD, 64), BF16),
        pltpu.VMEM((NCHAN, CD, 64), BF16),
        dma,
        dma((4,)), dma((4,)),
        dma((NZ,)), dma((NZ,)),
        dma((NZ,)), dma((NZ,)),
        dma((NZ,)), dma((NZ,)),
        dma((NZ,)), dma((NZ,)),
        dma((NZ,)), dma((NZ,)),
        dma((NZ,)), dma((NZ,)),
        dma((2 * NX,)), dma((2 * NX,)),
        dma, dma,
        dma((NCHAN,)), dma((NCHAN,)),
    ]
    return pl.pallas_call(
        kernel,
        out_shape=jax.ShapeDtypeStruct((C, 64), BF16),
        in_specs=[vmem, vmem, smem, smem, pl.BlockSpec(memory_space=pl.ANY), vmem, vmem, vmem, vmem],
        out_specs=vmem,
        scratch_shapes=scratch,
        compiler_params=pltpu.CompilerParams(
            collective_id=0, has_side_effects=True, vmem_limit_bytes=48 * 2**20
        ),
    )(
        features, positions, lists, counts, fourier_filter, radial_weights,
        norm_gain.reshape(1, C), mlp_in, mlp_out,
    )


def solution(mesh):
    return jax.shard_map(
        body,
        mesh=mesh,
        in_specs=(
            P("chan", "brick"),
            P(None, "brick"),
            P("brick", None),
            P("brick"),
            P("chan", None),
            P(None, "chan"),
            P(),
            P(None, "chan"),
            P("chan", None),
        ),
        out_specs=P(None, ("brick", "chan")),
        check_vma=False,
    )
```

```python
import math

import jax
import jax.numpy as jnp
from jax import lax
from jax.experimental import pallas as pl
from jax.experimental.pallas import tpu as pltpu
from jax.sharding import PartitionSpec as P

MESH = pl.DeviceIdType.MESH
F32 = jnp.float32
BF16 = jnp.bfloat16

NZ = 8
NY = 4
NX = 4
NBRICK = NZ * NY * 2
NCHAN = 8
CD = 64
AD = 512
AC = 2 * AD
C = 512
HID = 1024
NB = 8
KS = 16
WAVES = 2
WIDTH, CROSS, CUTOFF, EPS = 4.0, 8.0, 2.0, 1e-06
SPACING = CUTOFF / (NB - 1)
INVERSE = 1.0 / math.sqrt(AD * NBRICK)

NN = (((1,), (0,)), ((), ()))
NT = (((1,), (1,)), ((), ()))


def dot(a, b, dims):
    return lax.dot_general(a, b, dims, preferred_element_type=F32)


def turn(u):
    u = u - jnp.floor(u + 0.5)
    th = u * math.pi
    q = th * th
    s = -1.0 / 39916800
    for n in (362880, -5040, 120, -6, 1):
        s = s * q + 1.0 / n
    s = s * th
    c = 1.0 / 479001600
    for n in (-3628800, 40320, -720, 24, -2, 1):
        c = c * q + 1.0 / n
    return 1.0 - 2.0 * s * s, 2.0 * s * c


def kernel(
    feat_in, pos_in, lists_in, counts_in, filt, rw_in, gain_in, win_in, wout_in, out,
    fc, pc, lists, counts, rw, gain,
    ph, trig, uv, ff, ss, own_sum, rs1, t2, rs2, fg, flt,
    pt, sc, bas, msg, ew, ewr, wg, ms, mr,
    load_sem, sib_s, sib_r, halo_s, halo_r, rs1_s, rs1_r, rs2_s, rs2_r,
    ag1_s, ag1_r, ag2_s, ag2_r, ew_s, ew_r, w_s, w_r, wf_s, wf_r, a2a_s, a2a_r,
):
    brick = lax.axis_index("brick")
    chan = lax.axis_index("chan")
    core = lax.rem(brick, 2)
    z = lax.rem(brick // 2, NZ)
    y = brick // (2 * NZ)
    x = lax.rem(chan, NX)
    ylo = chan // NX
    first = core == 0
    second = core == 1
    kinds = ((0, first), (1, second))

    def at(yy, zz, cc):
        return ((lax.rem(yy, NY) * NZ + lax.rem(zz, NZ)) * 2 + cc, chan)

    sibling = at(y, z, 1 - core)
    beside = (lax.rem(brick + NBRICK + 2 * core - 1, NBRICK), chan)
    z_peer = lambda d: at(y, z + d, core)
    y_peer = lambda d: at(y + d, z, core)
    chan_peer = lambda d: (brick, lax.rem(chan + d, NCHAN))
    x_peer = lambda d: (brick, ylo * NX + lax.rem(x + d, NX))
    ylo_peer = (brick, (1 - ylo) * NX + x)

    barrier = pltpu.get_barrier_semaphore()
    partners = [z_peer(d) for d in range(1, NZ)] + [y_peer(d) for d in range(1, NY)]
    partners += [chan_peer(d) for d in range(1, NCHAN)] + [sibling, beside]
    for device in partners:
        pl.semaphore_signal(barrier, inc=1, device_id=device, device_id_type=MESH)

    loads = [(lists_in, lists), (counts_in, counts), (rw_in, rw), (gain_in, gain)]
    for pair_at in range(2):
        lanes = pl.ds(pair_at * 256, 256)
        loads.append((feat_in.at[:, lanes], fc.at[1 + 2 * core + pair_at]))
        loads.append((pos_in.at[:, lanes], pc.at[1 + 2 * core + pair_at]))
    own_unit = jnp.where(first, y, lax.rem(z, 4))
    own_nz = [jnp.where(first, 2 * z + w, 4 * y + 2 * w + z // 4) for w in range(WAVES)]
    for w in range(WAVES):
        rows = pl.ds(pl.multiple_of(lax.rem(own_unit, 2) * 32, 32), 32)
        lanes = pl.ds(pl.multiple_of(own_nz[w] * 256 + own_unit // 2 * 128, 128), 128)
        loads.append((filt.at[rows, lanes], flt.at[w]))
    loads = [pltpu.make_async_copy(a, b, load_sem.at[i]) for i, (a, b) in enumerate(loads)]
    for copy in loads:
        copy.start()
    weight_load = load_sem.at[len(loads)]

    @pl.when(first)
    def _():
        pltpu.make_async_copy(win_in, wg.at[core, chan], weight_load).start()

    @pl.when(second)
    def _():
        pltpu.make_async_copy(wout_in, wg.at[core, chan], weight_load).start()

    for copy in loads:
        copy.wait()
    pltpu.make_async_copy(wout_in, wg.at[core, chan], weight_load).wait()

    pl.semaphore_wait(barrier, len(partners))

    def remote(src, dst, send, recv, device):
        return pltpu.make_async_remote_copy(
            src_ref=src, dst_ref=dst, send_sem=send, recv_sem=recv,
            device_id=device, device_id_type=MESH,
        )

    places = pc.at[pl.ds(1 + 2 * core, 2)]
    block = fc.at[pl.ds(1 + 2 * core, 2)]
    to_sibling = [
        remote(places, places, sib_s.at[0], sib_r.at[0], sibling),
        remote(block, block, sib_s.at[1], sib_r.at[1], sibling),
    ]
    rim, land = jnp.where(first, 1, 4), jnp.where(first, 5, 0)
    halos = [
        remote(pc.at[rim], pc.at[land], halo_s.at[0], halo_r.at[0], beside),
        remote(fc.at[rim], fc.at[land], halo_s.at[1], halo_r.at[1], beside),
    ]
    mine = wg.at[core, chan]
    weight_y = remote(mine, mine, w_s.at[0], w_r.at[0], ylo_peer)
    weight_x = [remote(mine, mine, w_s.at[d], w_r.at[d], x_peer(d)) for d in range(1, NX)]
    for copy in to_sibling + halos + [weight_y] + weight_x:
        copy.start()

    number = lax.broadcasted_iota(jnp.int32, (KS, 1), 0).astype(F32)

    def dimension_phases(half):
        where = 1 + 2 * half
        for pair_at in range(2):
            spot = pc[where + pair_at]
            lanes = pl.ds(pl.multiple_of(half * 512 + pair_at * 256, 256), 256)
            px, py, pz = spot[0:1, :], spot[1:2, :], spot[2:3, :]
            xturn = ((brick - core + half).astype(F32) + px) * (1.0 / NBRICK)
            cx, sx = turn((number + 1.0) * xturn)
            cy, sy = turn((number - KS // 2) * py)
            cz, sz = turn((number - KS // 2) * pz)
            trig[0, :, lanes] = cz
            trig[1, :, lanes] = sz
            for r in range(KS):
                rows = slice(r * KS, (r + 1) * KS)
                even = cx * cy[r : r + 1, :] - sx * sy[r : r + 1, :]
                odd = sx * cy[r : r + 1, :] + cx * sy[r : r + 1, :]
                uv[0, rows, lanes] = jnp.where(first, even, odd)
                uv[1, rows, lanes] = jnp.where(first, -odd, even)

    dimension_phases(core)
    to_sibling[0].wait_recv()
    dimension_phases(1 - core)
    to_sibling[1].wait_recv()
    for pair_at in range(4):
        ff[:, pair_at * 256 : (pair_at + 1) * 256] = fc[1 + pair_at]
    features = ff[...]

    def rs1_copy(w, i):
        device = (
            jnp.where(first, at(y, z + i + 1, 0)[0], at(y + i // 2 + 1, z, 1)[0]),
            chan,
        )
        slot = w * NZ + i
        return remote(ss.at[slot], rs1.at[slot], rs1_s.at[slot], rs1_r.at[slot], device)

    def forward(step, carry):
        w, i = step // NZ, lax.rem(step, NZ)
        za = lax.rem(z + i + 1, NZ)
        yb = lax.rem(y + i // 2 + 1, NY)
        nz = jnp.where(first, 2 * za + w, 4 * yb + 2 * w + lax.rem(i, 2))
        cn, sn = trig[0, pl.ds(nz, 1), :], trig[1, pl.ds(nz, 1), :]
        for g in range(16):
            rows = slice(g * 16, (g + 1) * 16)
            ph[nz, rows, :] = (uv[0, rows, :] * cn + uv[1, rows, :] * sn).astype(BF16)
        total = dot(features, ph[nz], NT)
        ss[step] = total.astype(BF16)

        @pl.when(i < 7 - core)
        def _():
            rs1_copy(w, i).start()

        @pl.when(i >= 6)
        def _():
            own_sum[2 * w + i - 6] = total

        return carry

    lax.fori_loop(0, WAVES * NZ, forward, 0)

    weight_y.wait_recv()
    theirs = wg.at[core, (1 - ylo) * NX + x]
    weight_r = [
        remote(theirs, theirs, w_s.at[NX + d], w_r.at[NX + d], x_peer(d)) for d in range(1, NX)
    ]
    for copy in weight_r:
        copy.start()

    def make_sources():
        for copy in halos:
            copy.wait_recv()
        rw_pad = jnp.concatenate([rw[...], jnp.zeros((NB, CD), F32)], axis=1)
        rw_t = jnp.transpose(rw_pad)[0:CD, :]
        for e in range(8):
            lanes = slice((e % 2) * 128, (e % 2 + 1) * 128)
            shift = -1.0 if e < 2 else (1.0 if e >= 6 else 0.0)
            rows = jnp.concatenate(
                [pc[2 * core + e // 2, :, lanes], jnp.zeros((5, 128), F32)], axis=0
            )
            at_x = lax.broadcasted_iota(jnp.int32, (8, 128), 0) == 0
            pt[e] = jnp.transpose(jnp.where(at_x, rows + shift, rows))
            block = fc[2 * core + e // 2, :, lanes].astype(F32)
            for m in range(NB):
                sc[e, :, m * 128 : (m + 1) * 128] = (block * rw_t[:, m : m + 1]).astype(BF16)

    def message(t, l):
        e = lists[t, l]
        used = jnp.where(l < counts[t], 1.0, 0.0).astype(F32)
        source = pt[e]
        lane = slice((t % 2) * 128, (t % 2 + 1) * 128)
        target = pc[1 + 2 * core + t // 2, :, lane]
        dx = (source[:, 0:1] - target[0:1, :]) * WIDTH
        dy = (source[:, 1:2] - target[1:2, :]) * CROSS
        dz = (source[:, 2:3] - target[2:3, :]) * CROSS
        r2 = dx * dx + dy * dy + dz * dz
        env = jnp.maximum(1.0 - r2 * (1.0 / (CUTOFF * CUTOFF)), 0.0)
        tt = jnp.minimum(jnp.sqrt(r2) * (1.0 / SPACING), float(NB - 1))
        value = jnp.exp(-tt * tt) * (env * env * used)
        ratio = jnp.exp(2.0 * tt)
        bas[0:128, :] = value.astype(BF16)
        for m in range(1, NB):
            value = value * (ratio * math.exp(-(2 * m - 1)))
            bas[m * 128 : (m + 1) * 128, :] = value.astype(BF16)
        return dot(sc[e], bas[...], NN)

    def messages(t):
        msg[t] = lax.fori_loop(
            0, 4, lambda l, acc: acc + message(t, l), jnp.zeros((CD, 128), F32)
        )

    near = (NY, NZ)
    far = (NZ, NY)

    def near_device(d):
        return (jnp.where(first, at(y + d, z, 0)[0], at(y, z + d, 1)[0]), chan)

    def rs2_copy(w, d):
        unit = jnp.where(first, lax.rem(y + d, NY), lax.rem(z + d, NZ))
        slot = w * NZ + d
        return remote(
            t2.at[w, unit], rs2.at[slot], rs2_s.at[slot], rs2_r.at[slot], near_device(d)
        )

    def far_summed(w):
        for kind, here in kinds:

            @pl.when(here)
            def _():
                for i in range(NZ - 1 - kind):
                    rs1_copy(w, i).wait_recv()
                for h in range(1 + kind):
                    total = own_sum[2 * w + (h if kind else 1)]
                    for i in range(h, NZ - 1 - kind, 1 + kind):
                        total = total + rs1[w * NZ + i].astype(F32)
                    for u in range(4):
                        t2[w, 4 * h + u] = total[
                            32 * (u % 2) : 32 * (u % 2 + 1), 128 * (u // 2) : 128 * (u // 2 + 1)
                        ].astype(BF16)
                for d in range(1, near[kind]):
                    rs2_copy(w, d).start()

    def ag1_copy(w, d):
        unit = fg.at[own_nz[w], own_unit]
        slot = w * NZ + d
        return remote(unit, unit, ag1_s.at[slot], ag1_r.at[slot], near_device(d))

    def near_summed(w):
        for kind, here in kinds:

            @pl.when(here)
            def _():
                total = t2[w, z if kind else y].astype(F32)
                for d in range(1, near[kind]):
                    rs2_copy(w, d).wait_recv()
                    total = total + rs2[w * NZ + d].astype(F32)
                fg[own_nz[w], own_unit] = (flt[w] * (total * INVERSE)).astype(BF16)
                for d in range(1, near[kind]):
                    ag1_copy(w, d).start()

    def ag2_copy(kind, w, d):
        if kind == 0:
            group = fg.at[pl.ds(2 * z + w, 1)]
        else:
            group = fg.at[pl.ds(4 * y + 2 * w, 2)]
        slot = w * NZ + d
        device = (y_peer if kind else z_peer)(d)
        return remote(group, group, ag2_s.at[slot], ag2_r.at[slot], device)

    def near_gathered(w):
        for kind, here in kinds:

            @pl.when(here)
            def _():
                for d in range(1, near[kind]):
                    ag1_copy(w, d).wait_recv()
                for d in range(1, far[kind]):
                    ag2_copy(kind, w, d).start()

    def product(nz):
        top = jnp.concatenate([fg[nz, 0], fg[nz, 2]], axis=1)
        bottom = jnp.concatenate([fg[nz, 1], fg[nz, 3]], axis=1)
        return dot(jnp.concatenate([top, bottom], axis=0), ph[nz], NN)

    def evaluate(w, begin):
        for kind, here in kinds:

            @pl.when(here)
            def _():
                for i in range(4):
                    if kind == 0:
                        chunks = []
                        for d in (2 * i, 2 * i + 1):
                            if d:
                                ag2_copy(kind, w, d).wait_recv()
                            chunks.append(2 * lax.rem(z + NZ - d, NZ) + w)
                    else:
                        if i:
                            ag2_copy(kind, w, i).wait_recv()
                        base = 4 * lax.rem(y + NY - i, NY) + 2 * w
                        chunks = [base, base + 1]
                    total = product(chunks[0]) + product(chunks[1])
                    if begin and i == 0:
                        ew[0] = total[:, 0:AD]
                        ew[1] = total[:, AD:AC]
                    else:
                        ew[0] += total[:, 0:AD]
                        ew[1] += total[:, AD:AC]

    weights_on = remote(wg.at[core], wg.at[core], wf_s, wf_r, sibling)

    make_sources()
    far_summed(0)
    messages(0)
    far_summed(1)
    near_summed(0)
    messages(1)
    near_summed(1)
    near_gathered(0)
    messages(2)
    near_gathered(1)
    for copy in weight_x + weight_r:
        copy.wait_recv()
    weights_on.start()
    messages(3)
    evaluate(0, True)
    evaluate(1, False)

    ewald_share = remote(ew.at[1 - core], ewr, ew_s, ew_r, sibling)
    ewald_share.start()

    ewald_share.wait_recv()
    for t in range(4):
        lanes = slice(t * 128, (t + 1) * 128)
        pair_lanes = slice((t % 2) * 128, (t % 2 + 1) * 128)
        ewald = (ew[core, :, lanes] + ewr[:, lanes]) * INVERSE
        mixed = (
            fc[1 + 2 * core + t // 2, :, pair_lanes].astype(F32) + msg[t] + ewald
        ).astype(BF16)
        ms[2 * t] = mixed[:, 0:64]
        ms[2 * t + 1] = mixed[:, 64:128]
    exchange = []
    for d in range(1, NCHAN):
        device = chan_peer(d)
        exchange.append(
            remote(ms.at[device[1]], mr.at[chan], a2a_s.at[d], a2a_r.at[d], device)
        )
        exchange[-1].start()
    mr[chan] = ms[chan]
    remote(wg.at[1 - core], wg.at[1 - core], wf_s, wf_r, sibling).wait_recv()
    for copy in exchange:
        copy.wait_recv()

    eye = (
        lax.broadcasted_iota(jnp.int32, (64, 64), 0)
        == lax.broadcasted_iota(jnp.int32, (64, 64), 1)
    ).astype(BF16)
    values = dot(eye, mr[...].reshape(C, 64), NT)
    mean_square = jnp.sum(values * values, axis=1, keepdims=True) * (1.0 / C)
    normed = (values * lax.rsqrt(mean_square + EPS) * gain[...]).astype(BF16)
    hidden = dot(normed, wg[0].reshape(C, HID), NN)
    active = jax.nn.gelu(hidden).astype(BF16)
    out[...] = (values + dot(active, wg[1].reshape(C, HID), NT)).astype(BF16)

    for copy in to_sibling + halos + weight_x + weight_r + [weight_y, weights_on, ewald_share]:
        copy.wait_send()
    for copy in exchange:
        copy.wait_send()
    for kind, here in kinds:

        @pl.when(here)
        def _():
            for w in range(WAVES):
                for i in range(NZ - 1 - kind):
                    rs1_copy(w, i).wait_send()
                for d in range(1, near[kind]):
                    rs2_copy(w, d).wait_send()
                    ag1_copy(w, d).wait_send()
                for d in range(1, far[kind]):
                    ag2_copy(kind, w, d).wait_send()


def body(features, positions, lists, counts, fourier_filter, radial_weights, norm_gain, mlp_in, mlp_out):
    dma = pltpu.SemaphoreType.DMA
    slots = WAVES * NZ
    scratch = [
        pltpu.VMEM((6, CD, 256), BF16),
        pltpu.VMEM((6, 3, 256), F32),
        pltpu.SMEM((4, 4), jnp.int32),
        pltpu.SMEM((4,), jnp.int32),
        pltpu.VMEM((NB, CD), F32),
        pltpu.VMEM((1, C), F32),
        pltpu.VMEM((KS, 256, AC), BF16),
        pltpu.VMEM((2, KS, AC), F32),
        pltpu.VMEM((2, 256, AC), F32),
        pltpu.VMEM((CD, AC), BF16),
        pltpu.VMEM((slots, CD, 256), BF16),
        pltpu.VMEM((2 * WAVES, CD, 256), F32),
        pltpu.VMEM((slots, CD, 256), BF16),
        pltpu.VMEM((WAVES, NZ, 32, 128), BF16),
        pltpu.VMEM((slots, 32, 128), BF16),
        pltpu.VMEM((KS, 4, 32, 128), BF16),
        pltpu.VMEM((WAVES, 32, 128), F32),
        pltpu.VMEM((8, 128, 8), F32),
        pltpu.VMEM((8, CD, NB * 128), BF16),
        pltpu.VMEM((NB * 128, 128), BF16),
        pltpu.VMEM((4, CD, 128), F32),
        pltpu.VMEM((2, CD, AD), F32),
        pltpu.VMEM((CD, AD), F32),
        pltpu.VMEM((2, NCHAN, CD, HID), BF16),
        pltpu.VMEM((NCHAN, CD, 64), BF16),
        pltpu.VMEM((NCHAN, CD, 64), BF16),
        dma((11,)),
        dma((2,)), dma((2,)),
        dma((2,)), dma((2,)),
        dma((slots,)), dma((slots,)),
        dma((slots,)), dma((slots,)),
        dma((slots,)), dma((slots,)),
        dma((slots,)), dma((slots,)),
        dma, dma,
        dma((2 * NX,)), dma((2 * NX,)),
        dma, dma,
        dma((NCHAN,)), dma((NCHAN,)),
    ]
    return pl.pallas_call(
        kernel,
        out_shape=jax.ShapeDtypeStruct((64, C), BF16),
        in_specs=[pl.BlockSpec(memory_space=pltpu.HBM)] * 9,
        out_specs=pl.BlockSpec(memory_space=pltpu.VMEM),
        scratch_shapes=scratch,
        compiler_params=pltpu.CompilerParams(
            collective_id=0, has_side_effects=True, vmem_limit_bytes=60 * 2**20
        ),
    )(
        features, positions, lists, counts, fourier_filter, radial_weights,
        norm_gain.reshape(1, C), mlp_in.T, mlp_out,
    ).T


def solution(mesh):
    return jax.shard_map(
        body,
        mesh=mesh,
        in_specs=(
            P("chan", "brick"),
            P(None, "brick"),
            P("brick", None),
            P("brick"),
            P("chan", None),
            P(None, "chan"),
            P(),
            P(None, "chan"),
            P("chan", None),
        ),
        out_specs=P(None, ("brick", "chan")),
        check_vma=False,
    )
```

```python
import math

import jax
import jax.numpy as jnp
from jax import lax
from jax.experimental import pallas as pl
from jax.experimental.pallas import tpu as pltpu
from jax.sharding import PartitionSpec as P

MESH = pl.DeviceIdType.MESH
F32 = jnp.float32
BF16 = jnp.bfloat16

NZ = 8
NY = 4
NX = 4
NBRICK = NZ * NY * 2
NCHAN = 8
CD = 64
AD = 512
C = 512
HID = 1024
NB = 8
KS = 16
WAVES = 2
WIDTH, CROSS, CUTOFF, EPS = 4.0, 8.0, 2.0, 1e-06
SPACING = CUTOFF / (NB - 1)
INVERSE = 1.0 / math.sqrt(AD * NBRICK)

NN = (((1,), (0,)), ((), ()))
NT = (((1,), (1,)), ((), ()))


FAR_Z = (4, 3, 5, 2, 6, 1, 7)
FAR_Y = (2, 1, 3)
FAR_CHAN = ((1, 2), (1, 1), (1, 3), (0, 2), (1, 0), (0, 1), (0, 3))


def dot(a, b, dims):
    return lax.dot_general(a, b, dims, preferred_element_type=F32)


def turn(u):
    u = u - jnp.floor(u + 0.5)
    th = u * math.pi
    q = th * th
    s = -1.0 / 39916800
    for n in (362880, -5040, 120, -6, 1):
        s = s * q + 1.0 / n
    s = s * th
    c = 1.0 / 479001600
    for n in (-3628800, 40320, -720, 24, -2, 1):
        c = c * q + 1.0 / n
    return 1.0 - 2.0 * s * s, 2.0 * s * c


def kernel(
    feat_in, pos_in, lists_in, counts_in, filt, rw_in, gain_in, win_in, wout_in, out,
    fc, pc, lists, counts, rw, gain,
    ph, trig, uv, ff, ss, own_sum, rs1, t2, rs2, fg, flt,
    pt, sc, bas, msg, ew, ewr, wg, ms, mr,
    load_sem, sib_s, sib_r, halo_s, halo_r, rs1_s, rs1_r, rs2_s, rs2_r,
    ag1_s, ag1_r, ag2_s, ag2_r, ew_s, ew_r, w_s, w_r, wf_s, wf_r, a2a_s, a2a_r,
):
    brick = lax.axis_index("brick")
    chan = lax.axis_index("chan")
    core = lax.rem(brick, 2)
    z = lax.rem(brick // 2, NZ)
    y = brick // (2 * NZ)
    x = lax.rem(chan, NX)
    ylo = chan // NX
    first = core == 0
    second = core == 1
    kinds = ((0, first), (1, second))

    def at(yy, zz, cc):
        return ((lax.rem(yy, NY) * NZ + lax.rem(zz, NZ)) * 2 + cc, chan)

    sibling = at(y, z, 1 - core)
    beside = (lax.rem(brick + NBRICK + 2 * core - 1, NBRICK), chan)
    z_peer = lambda d: at(y, z + d, core)
    y_peer = lambda d: at(y + d, z, core)
    chan_peer = lambda d: (brick, lax.rem(chan + d, NCHAN))
    x_peer = lambda d: (brick, ylo * NX + lax.rem(x + d, NX))
    ylo_peer = (brick, (1 - ylo) * NX + x)

    loads = []
    for pair_at in range(2):
        lanes = pl.ds(pair_at * 256, 256)
        loads.append((pos_in.at[:, lanes], pc.at[1 + 2 * core + pair_at]))
        loads.append((feat_in.at[:, lanes], fc.at[1 + 2 * core + pair_at]))
        loads.append((feat_in.at[:, lanes], ff.at[core, :, lanes]))
    urgent = len(loads)
    loads += [(lists_in, lists), (counts_in, counts), (rw_in, rw), (gain_in, gain)]
    own_unit = jnp.where(first, y, lax.rem(z, 4))
    own_nz = [jnp.where(first, 2 * z + w, 4 * y + 2 * w + z // 4) for w in range(WAVES)]
    for w in range(WAVES):
        rows = pl.ds(pl.multiple_of(lax.rem(own_unit, 2) * 32, 32), 32)
        lanes = pl.ds(pl.multiple_of(own_nz[w] * 256 + own_unit // 2 * 128, 128), 128)
        loads.append((filt.at[rows, lanes], flt.at[w]))
    loads = [pltpu.make_async_copy(a, b, load_sem.at[i]) for i, (a, b) in enumerate(loads)]
    for copy in loads:
        copy.start()
    weight_load = load_sem.at[len(loads)]

    @pl.when(first)
    def _():
        pltpu.make_async_copy(win_in, wg.at[core, chan], weight_load).start()

    @pl.when(second)
    def _():
        pltpu.make_async_copy(wout_in, wg.at[core, chan], weight_load).start()

    barrier = pltpu.get_barrier_semaphore()
    partners = [sibling, beside] + [z_peer(d) for d in FAR_Z] + [y_peer(d) for d in FAR_Y]
    partners += [chan_peer(d) for d in range(1, NCHAN)]
    for device in partners:
        pl.semaphore_signal(barrier, inc=1, device_id=device, device_id_type=MESH)

    number = lax.broadcasted_iota(jnp.int32, (KS, 1), 0).astype(F32)

    def dimension_phases(half):
        for pair_at in range(2):
            spot = pc[1 + 2 * half + pair_at]
            lanes = pl.ds(pl.multiple_of(half * AD + pair_at * 256, 256), 256)
            px, py, pz = spot[0:1, :], spot[1:2, :], spot[2:3, :]
            xturn = ((brick - core + half).astype(F32) + px) * (1.0 / NBRICK)
            cx, sx = turn((number + 1.0) * xturn)
            cy, sy = turn((number - KS // 2) * py)
            cz, sz = turn((number - KS // 2) * pz)
            trig[0, :, lanes] = cz
            trig[1, :, lanes] = sz
            for r in range(KS):
                rows = slice(r * KS, (r + 1) * KS)
                even = cx * cy[r : r + 1, :] - sx * sy[r : r + 1, :]
                odd = sx * cy[r : r + 1, :] + cx * sy[r : r + 1, :]
                uv[0, rows, lanes] = jnp.where(first, even, odd)
                uv[1, rows, lanes] = jnp.where(first, -odd, even)

    def z_ahead(i):
        return 4 + jnp.where(lax.rem(i, 2) == 1, -((i + 1) // 2), i // 2)

    def y_ahead(i):
        k = i // 2
        return 2 + jnp.where(lax.rem(k, 2) == 1, -((k + 1) // 2), k // 2)

    def wave_number(step):
        w, i = step // NZ, lax.rem(step, NZ)
        za = lax.rem(z + z_ahead(i), NZ)
        yb = lax.rem(y + y_ahead(i), NY)
        return jnp.where(first, 2 * za + w, 4 * yb + 2 * w + lax.rem(i, 2))

    for copy in loads[:urgent]:
        copy.wait()
    for copy in loads[urgent:]:
        copy.wait()
    pltpu.make_async_copy(wout_in, wg.at[core, chan], weight_load).wait()

    pl.semaphore_wait(barrier, len(partners))

    def remote(src, dst, send, recv, device):
        return pltpu.make_async_remote_copy(
            src_ref=src, dst_ref=dst, send_sem=send, recv_sem=recv,
            device_id=device, device_id_type=MESH,
        )

    places = pc.at[pl.ds(1 + 2 * core, 2)]
    near_rim = 2 + core
    to_sibling = [
        remote(places, places, sib_s.at[0], sib_r.at[0], sibling),
        remote(ff.at[core], ff.at[core], sib_s.at[1], sib_r.at[1], sibling),
        remote(fc.at[near_rim], fc.at[near_rim], sib_s.at[2], sib_r.at[2], sibling),
    ]
    rim, land = jnp.where(first, 1, 4), jnp.where(first, 5, 0)
    halos = [
        remote(pc.at[rim], pc.at[land], halo_s.at[0], halo_r.at[0], beside),
        remote(fc.at[rim], fc.at[land], halo_s.at[1], halo_r.at[1], beside),
    ]
    mine = wg.at[core, chan]
    weight_y = remote(mine, mine, w_s.at[0], w_r.at[0], ylo_peer)
    weight_x = [remote(mine, mine, w_s.at[d], w_r.at[d], x_peer(d)) for d in range(1, NX)]
    for copy in to_sibling + halos + [weight_y] + weight_x:
        copy.start()

    dimension_phases(core)
    to_sibling[0].wait_recv()
    dimension_phases(1 - core)
    to_sibling[1].wait_recv()
    features = jnp.concatenate([ff[0], ff[1]], axis=1)

    def rs1_copy(w, i):
        device = (
            jnp.where(first, at(y, z + z_ahead(i), 0)[0], at(y + y_ahead(i), z, 1)[0]),
            chan,
        )
        slot = w * NZ + i
        return remote(ss.at[slot], rs1.at[slot], rs1_s.at[slot], rs1_r.at[slot], device)

    def forward(step, carry):
        w, i = step // NZ, lax.rem(step, NZ)
        nz = wave_number(step)
        cn, sn = trig[0, pl.ds(nz, 1), :], trig[1, pl.ds(nz, 1), :]
        for g in range(16):
            rows = slice(g * 16, (g + 1) * 16)
            ph[nz, rows, :] = (uv[0, rows, :] * cn + uv[1, rows, :] * sn).astype(BF16)
        total = dot(features, ph[nz], NT)
        ss[step] = total.astype(BF16)

        @pl.when(i < 7 - core)
        def _():
            rs1_copy(w, i).start()

        @pl.when(i >= 6)
        def _():
            own_sum[2 * w + i - 6] = total

        return carry

    lax.fori_loop(0, WAVES * NZ, forward, 0)

    weight_y.wait_recv()
    theirs = wg.at[core, (1 - ylo) * NX + x]
    weight_r = [
        remote(theirs, theirs, w_s.at[NX + d], w_r.at[NX + d], x_peer(d)) for d in range(1, NX)
    ]
    for copy in weight_r:
        copy.start()

    def make_sources():
        for copy in halos + to_sibling[2:]:
            copy.wait_recv()
        msg[...] = jnp.zeros((4, CD, 128), F32)
        rw_pad = jnp.concatenate([rw[...], jnp.zeros((NB, CD), F32)], axis=1)
        rw_t = jnp.transpose(rw_pad)[0:CD, :]
        for e in range(8):
            lanes = slice((e % 2) * 128, (e % 2 + 1) * 128)
            shift = -1.0 if e < 2 else (1.0 if e >= 6 else 0.0)
            rows = jnp.concatenate(
                [pc[2 * core + e // 2, :, lanes], jnp.zeros((5, 128), F32)], axis=0
            )
            at_x = lax.broadcasted_iota(jnp.int32, (8, 128), 0) == 0
            pt[e] = jnp.transpose(jnp.where(at_x, rows + shift, rows))
            block = fc[2 * core + e // 2, :, lanes].astype(F32)
            for m in range(NB):
                sc[e, :, m * 128 : (m + 1) * 128] = (block * rw_t[:, m : m + 1]).astype(BF16)

    def message(t, l):
        e = lists[t, l]
        used = jnp.where(l < counts[t], 1.0, 0.0).astype(F32)
        source = pt[e]
        lane = pl.ds(pl.multiple_of(lax.rem(t, 2) * 128, 128), 128)
        target = pc[1 + 2 * core + t // 2, :, lane]
        dx = (source[:, 0:1] - target[0:1, :]) * WIDTH
        dy = (source[:, 1:2] - target[1:2, :]) * CROSS
        dz = (source[:, 2:3] - target[2:3, :]) * CROSS
        r2 = dx * dx + dy * dy + dz * dz
        env = jnp.maximum(1.0 - r2 * (1.0 / (CUTOFF * CUTOFF)), 0.0)
        tt = jnp.minimum(jnp.sqrt(r2) * (1.0 / SPACING), float(NB - 1))
        value = jnp.exp(-tt * tt) * (env * env * used)
        ratio = jnp.exp(2.0 * tt)
        bas[0:128, :] = value.astype(BF16)
        for m in range(1, NB):
            value = value * (ratio * math.exp(-(2 * m - 1)))
            bas[m * 128 : (m + 1) * 128, :] = value.astype(BF16)
        return dot(sc[e], bas[...], NN)

    def messages(begin, end):
        def entry(k, carry):
            t = k // 4
            msg[t] += message(t, lax.rem(k, 4))
            return carry

        lax.fori_loop(begin, end, entry, 0)

    near = (FAR_Y, FAR_Z)
    far = (FAR_Z, FAR_Y)

    def near_device(d):
        return (jnp.where(first, at(y + d, z, 0)[0], at(y, z + d, 1)[0]), chan)

    def rs2_copy(w, d):
        unit = jnp.where(first, lax.rem(y + d, NY), lax.rem(z + d, NZ))
        slot = w * NZ + d
        return remote(
            t2.at[w, unit], rs2.at[slot], rs2_s.at[slot], rs2_r.at[slot], near_device(d)
        )

    def far_summed(w):
        for kind, here in kinds:

            @pl.when(here)
            def _():
                for i in range(NZ - 1 - kind):
                    rs1_copy(w, i).wait_recv()
                for h in range(1 + kind):
                    total = own_sum[2 * w + (h if kind else 1)]
                    for i in range(h, NZ - 1 - kind, 1 + kind):
                        total = total + rs1[w * NZ + i].astype(F32)
                    for u in range(4):
                        t2[w, 4 * h + u] = total[
                            32 * (u % 2) : 32 * (u % 2 + 1), 128 * (u // 2) : 128 * (u // 2 + 1)
                        ].astype(BF16)
                for d in near[kind]:
                    rs2_copy(w, d).start()

    def ag1_copy(w, d):
        unit = fg.at[own_nz[w], own_unit]
        slot = w * NZ + d
        return remote(unit, unit, ag1_s.at[slot], ag1_r.at[slot], near_device(d))

    def near_summed(w):
        for kind, here in kinds:

            @pl.when(here)
            def _():
                total = t2[w, z if kind else y].astype(F32)
                for d in near[kind]:
                    rs2_copy(w, d).wait_recv()
                    total = total + rs2[w * NZ + d].astype(F32)
                fg[own_nz[w], own_unit] = (flt[w] * (total * INVERSE)).astype(BF16)
                for d in near[kind]:
                    ag1_copy(w, d).start()

    def ag2_copy(kind, w, d):
        if kind == 0:
            group = fg.at[pl.ds(2 * z + w, 1)]
        else:
            group = fg.at[pl.ds(4 * y + 2 * w, 2)]
        slot = w * NZ + d
        device = (y_peer if kind else z_peer)(d)
        return remote(group, group, ag2_s.at[slot], ag2_r.at[slot], device)

    def near_gathered(w):
        for kind, here in kinds:

            @pl.when(here)
            def _():
                for d in near[kind]:
                    ag1_copy(w, d).wait_recv()
                for d in far[kind]:
                    ag2_copy(kind, w, d).start()

    def filtered(nz):
        top = jnp.concatenate([fg[nz, 0], fg[nz, 2]], axis=1)
        bottom = jnp.concatenate([fg[nz, 1], fg[nz, 3]], axis=1)
        return jnp.concatenate([top, bottom], axis=0)

    ewald_share = remote(ew.at[1 - core], ewr, ew_s, ew_r, sibling)

    def evaluate(w):
        for kind, here in kinds:

            @pl.when(here)
            def _():
                for i in range(4):
                    if kind == 0:
                        chunks = []
                        for d in ((0, 1), (7, 2), (6, 3), (5, 4))[i]:
                            if d:
                                ag2_copy(kind, w, d).wait_recv()
                            chunks.append(2 * lax.rem(z + NZ - d, NZ) + w)
                    else:
                        d = (0, 1, 3, 2)[i]
                        if d:
                            ag2_copy(kind, w, d).wait_recv()
                        base = 4 * lax.rem(y + NY - d, NY) + 2 * w
                        chunks = [base, base + 1]
                    total = sum(dot(filtered(nz), ph[nz], NN) for nz in chunks)
                    for half in range(2):
                        lanes = slice(half * AD, (half + 1) * AD)
                        if w == 0 and i == 0:
                            ew[half] = total[:, lanes]
                        else:
                            ew[half] += total[:, lanes]

    weights_on = remote(wg.at[core], wg.at[core], wf_s, wf_r, sibling)

    make_sources()
    far_summed(0)
    messages(0, 3)
    far_summed(1)
    messages(3, 6)
    near_summed(0)
    messages(6, 10)
    near_summed(1)
    messages(10, 13)
    near_gathered(0)
    messages(13, 16)
    near_gathered(1)
    for copy in weight_x + weight_r:
        copy.wait_recv()
    weights_on.start()
    evaluate(0)
    evaluate(1)
    ewald_share.start()

    ewald_share.wait_recv()
    for t in range(4):
        lanes = slice(t * 128, (t + 1) * 128)
        pair_lanes = slice((t % 2) * 128, (t % 2 + 1) * 128)
        ewald = (ew[core, :, lanes] + ewr[:, lanes]) * INVERSE
        mixed = (
            fc[1 + 2 * core + t // 2, :, pair_lanes].astype(F32) + msg[t] + ewald
        ).astype(BF16)
        ms[2 * t] = mixed[:, 0:64]
        ms[2 * t + 1] = mixed[:, 64:128]
    exchange = []
    for i, (dy, dx) in enumerate(FAR_CHAN):
        device = (brick, lax.rem(ylo + dy, 2) * NX + lax.rem(x + dx, NX))
        exchange.append(
            remote(ms.at[device[1]], mr.at[chan], a2a_s.at[i], a2a_r.at[i], device)
        )
        exchange[-1].start()
    mr[chan] = ms[chan]
    remote(wg.at[1 - core], wg.at[1 - core], wf_s, wf_r, sibling).wait_recv()
    for copy in exchange:
        copy.wait_recv()

    eye = (
        lax.broadcasted_iota(jnp.int32, (64, 64), 0)
        == lax.broadcasted_iota(jnp.int32, (64, 64), 1)
    ).astype(BF16)
    values = dot(eye, mr[...].reshape(C, 64), NT)
    mean_square = jnp.sum(values * values, axis=1, keepdims=True) * (1.0 / C)
    normed = (values * lax.rsqrt(mean_square + EPS) * gain[...]).astype(BF16)
    hidden = dot(normed, wg[0].reshape(C, HID), NN)
    active = jax.nn.gelu(hidden).astype(BF16)
    out[...] = (values + dot(active, wg[1].reshape(C, HID), NT)).astype(BF16)

    for copy in to_sibling + halos + weight_x + weight_r + [weight_y, weights_on, ewald_share]:
        copy.wait_send()
    for copy in exchange:
        copy.wait_send()
    for kind, here in kinds:

        @pl.when(here)
        def _():
            for w in range(WAVES):
                for i in range(NZ - 1 - kind):
                    rs1_copy(w, i).wait_send()
                for d in near[kind]:
                    rs2_copy(w, d).wait_send()
                    ag1_copy(w, d).wait_send()
                for d in far[kind]:
                    ag2_copy(kind, w, d).wait_send()


def body(features, positions, lists, counts, fourier_filter, radial_weights, norm_gain, mlp_in, mlp_out):
    dma = pltpu.SemaphoreType.DMA
    slots = WAVES * NZ
    scratch = [
        pltpu.VMEM((6, CD, 256), BF16),
        pltpu.VMEM((6, 3, 256), F32),
        pltpu.SMEM((4, 4), jnp.int32),
        pltpu.SMEM((4,), jnp.int32),
        pltpu.VMEM((NB, CD), F32),
        pltpu.VMEM((1, C), F32),
        pltpu.VMEM((KS, 256, 2 * AD), BF16),
        pltpu.VMEM((2, KS, 2 * AD), F32),
        pltpu.VMEM((2, 256, 2 * AD), F32),
        pltpu.VMEM((2, CD, AD), BF16),
        pltpu.VMEM((slots, CD, 256), BF16),
        pltpu.VMEM((2 * WAVES, CD, 256), F32),
        pltpu.VMEM((slots, CD, 256), BF16),
        pltpu.VMEM((WAVES, NZ, 32, 128), BF16),
        pltpu.VMEM((slots, 32, 128), BF16),
        pltpu.VMEM((KS, 4, 32, 128), BF16),
        pltpu.VMEM((WAVES, 32, 128), F32),
        pltpu.VMEM((8, 128, 8), F32),
        pltpu.VMEM((8, CD, NB * 128), BF16),
        pltpu.VMEM((NB * 128, 128), BF16),
        pltpu.VMEM((4, CD, 128), F32),
        pltpu.VMEM((2, CD, AD), F32),
        pltpu.VMEM((CD, AD), F32),
        pltpu.VMEM((2, NCHAN, CD, HID), BF16),
        pltpu.VMEM((NCHAN, CD, 64), BF16),
        pltpu.VMEM((NCHAN, CD, 64), BF16),
        dma((13,)),
        dma((3,)), dma((3,)),
        dma((2,)), dma((2,)),
        dma((slots,)), dma((slots,)),
        dma((slots,)), dma((slots,)),
        dma((slots,)), dma((slots,)),
        dma((slots,)), dma((slots,)),
        dma, dma,
        dma((2 * NX,)), dma((2 * NX,)),
        dma, dma,
        dma((NCHAN,)), dma((NCHAN,)),
    ]
    return pl.pallas_call(
        kernel,
        out_shape=jax.ShapeDtypeStruct((64, C), BF16),
        in_specs=[pl.BlockSpec(memory_space=pltpu.HBM)] * 9,
        out_specs=pl.BlockSpec(memory_space=pltpu.VMEM),
        scratch_shapes=scratch,
        compiler_params=pltpu.CompilerParams(
            collective_id=0, has_side_effects=True, vmem_limit_bytes=60 * 2**20
        ),
    )(
        features, positions, lists, counts, fourier_filter, radial_weights,
        norm_gain.reshape(1, C), mlp_in.T, mlp_out,
    ).T


def solution(mesh):
    return jax.shard_map(
        body,
        mesh=mesh,
        in_specs=(
            P("chan", "brick"),
            P(None, "brick"),
            P("brick", None),
            P("brick"),
            P("chan", None),
            P(None, "chan"),
            P(),
            P(None, "chan"),
            P("chan", None),
        ),
        out_specs=P(None, ("brick", "chan")),
        check_vma=False,
    )
```

```python
import math

import jax
import jax.numpy as jnp
from jax import lax
from jax.experimental import pallas as pl
from jax.experimental.pallas import tpu as pltpu
from jax.sharding import PartitionSpec as P

MESH = pl.DeviceIdType.MESH
F32 = jnp.float32
BF16 = jnp.bfloat16

NZ = 8
NY = 4
NX = 4
NBRICK = NZ * NY * 2
NCHAN = 8
CD = 64
AD = 512
C = 512
HID = 1024
NB = 8
KS = 16
WAVES = 2
WIDTH, CROSS, CUTOFF, EPS = 4.0, 8.0, 2.0, 1e-06
SPACING = CUTOFF / (NB - 1)
INVERSE = 1.0 / math.sqrt(AD * NBRICK)

NN = (((1,), (0,)), ((), ()))
NT = (((1,), (1,)), ((), ()))


FAR_Z = (4, 3, 5, 2, 6, 1, 7)
FAR_Y = (2, 1, 3)
FAR_CHAN = ((1, 2), (1, 1), (1, 3), (0, 2), (1, 0), (0, 1), (0, 3))


def dot(a, b, dims):
    return lax.dot_general(a, b, dims, preferred_element_type=F32)


def turn(u):
    u = u - jnp.floor(u + 0.5)
    th = u * math.pi
    q = th * th
    s = -1.0 / 39916800
    for n in (362880, -5040, 120, -6, 1):
        s = s * q + 1.0 / n
    s = s * th
    c = 1.0 / 479001600
    for n in (-3628800, 40320, -720, 24, -2, 1):
        c = c * q + 1.0 / n
    return 1.0 - 2.0 * s * s, 2.0 * s * c


def kernel(
    feat_in, pos_in, lists_in, counts_in, filt, rw_in, gain_in, win_in, wout_in, out,
    fc, pc, lists, counts, rw, gain,
    ph, trig, uv, ff, ss, own_sum, rs1, t2, rs2, fg, flt,
    pt, sc, bas, msg, ew, ewr, wg, ms, mr,
    load_sem, sib_s, sib_r, halo_s, halo_r, rs1_s, rs1_r, rs2_s, rs2_r,
    ag1_s, ag1_r, ag2_s, ag2_r, ew_s, ew_r, w_s, w_r, wf_s, wf_r, a2a_s, a2a_r,
):
    brick = lax.axis_index("brick")
    chan = lax.axis_index("chan")
    core = lax.rem(brick, 2)
    z = lax.rem(brick // 2, NZ)
    y = brick // (2 * NZ)
    x = lax.rem(chan, NX)
    ylo = chan // NX
    first = core == 0
    second = core == 1
    kinds = ((0, first), (1, second))

    def at(yy, zz, cc):
        return ((lax.rem(yy, NY) * NZ + lax.rem(zz, NZ)) * 2 + cc, chan)

    sibling = at(y, z, 1 - core)
    beside = (lax.rem(brick + NBRICK + 2 * core - 1, NBRICK), chan)
    z_peer = lambda d: at(y, z + d, core)
    y_peer = lambda d: at(y + d, z, core)
    chan_peer = lambda d: (brick, lax.rem(chan + d, NCHAN))
    x_peer = lambda d: (brick, ylo * NX + lax.rem(x + d, NX))
    ylo_peer = (brick, (1 - ylo) * NX + x)

    loads = []
    for pair_at in range(2):
        lanes = pl.ds(pair_at * 256, 256)
        loads.append((pos_in.at[:, lanes], pc.at[1 + 2 * core + pair_at]))
        loads.append((feat_in.at[:, lanes], fc.at[1 + 2 * core + pair_at]))
        loads.append((feat_in.at[:, lanes], ff.at[core, :, lanes]))
    urgent = len(loads)
    loads += [(lists_in, lists), (counts_in, counts), (rw_in, rw), (gain_in, gain)]
    own_unit = jnp.where(first, y, lax.rem(z, 4))
    own_nz = [jnp.where(first, 2 * z + w, 4 * y + 2 * w + z // 4) for w in range(WAVES)]
    for w in range(WAVES):
        rows = pl.ds(pl.multiple_of(lax.rem(own_unit, 2) * 32, 32), 32)
        lanes = pl.ds(pl.multiple_of(own_nz[w] * 256 + own_unit // 2 * 128, 128), 128)
        loads.append((filt.at[rows, lanes], flt.at[w]))
    loads = [pltpu.make_async_copy(a, b, load_sem.at[i]) for i, (a, b) in enumerate(loads)]
    for copy in loads:
        copy.start()
    weight_load = load_sem.at[len(loads)]

    @pl.when(first)
    def _():
        pltpu.make_async_copy(win_in, wg.at[core, chan], weight_load).start()

    @pl.when(second)
    def _():
        pltpu.make_async_copy(wout_in, wg.at[core, chan], weight_load).start()

    barrier = pltpu.get_barrier_semaphore()
    partners = [sibling, beside] + [z_peer(d) for d in FAR_Z] + [y_peer(d) for d in FAR_Y]
    partners += [chan_peer(d) for d in range(1, NCHAN)]
    for device in partners:
        pl.semaphore_signal(barrier, inc=1, device_id=device, device_id_type=MESH)

    number = lax.broadcasted_iota(jnp.int32, (KS, 1), 0).astype(F32)

    def dimension_phases(half):
        for pair_at in range(2):
            spot = pc[1 + 2 * half + pair_at]
            lanes = pl.ds(pl.multiple_of(half * AD + pair_at * 256, 256), 256)
            px, py, pz = spot[0:1, :], spot[1:2, :], spot[2:3, :]
            xturn = ((brick - core + half).astype(F32) + px) * (1.0 / NBRICK)
            cx, sx = turn((number + 1.0) * xturn)
            cy, sy = turn((number - KS // 2) * py)
            cz, sz = turn((number - KS // 2) * pz)
            trig[0, :, lanes] = cz
            trig[1, :, lanes] = sz
            for r in range(KS):
                rows = slice(r * KS, (r + 1) * KS)
                even = cx * cy[r : r + 1, :] - sx * sy[r : r + 1, :]
                odd = sx * cy[r : r + 1, :] + cx * sy[r : r + 1, :]
                uv[0, rows, lanes] = jnp.where(first, even, odd)
                uv[1, rows, lanes] = jnp.where(first, -odd, even)

    def z_ahead(i):
        return 4 + jnp.where(lax.rem(i, 2) == 1, -((i + 1) // 2), i // 2)

    def y_ahead(i):
        k = i // 2
        return 2 + jnp.where(lax.rem(k, 2) == 1, -((k + 1) // 2), k // 2)

    def wave_number(step):
        w, i = step // NZ, lax.rem(step, NZ)
        za = lax.rem(z + z_ahead(i), NZ)
        yb = lax.rem(y + y_ahead(i), NY)
        return jnp.where(first, 2 * za + w, 4 * yb + 2 * w + lax.rem(i, 2))

    for copy in loads[:urgent]:
        copy.wait()

    pl.semaphore_wait(barrier, len(partners))

    def remote(src, dst, send, recv, device):
        return pltpu.make_async_remote_copy(
            src_ref=src, dst_ref=dst, send_sem=send, recv_sem=recv,
            device_id=device, device_id_type=MESH,
        )

    places = pc.at[pl.ds(1 + 2 * core, 2)]
    near_rim = 2 + core
    to_sibling = [
        remote(places, places, sib_s.at[0], sib_r.at[0], sibling),
        remote(ff.at[core], ff.at[core], sib_s.at[1], sib_r.at[1], sibling),
        remote(fc.at[near_rim], fc.at[near_rim], sib_s.at[2], sib_r.at[2], sibling),
    ]
    rim, land = jnp.where(first, 1, 4), jnp.where(first, 5, 0)
    halos = [
        remote(pc.at[rim], pc.at[land], halo_s.at[0], halo_r.at[0], beside),
        remote(fc.at[rim], fc.at[land], halo_s.at[1], halo_r.at[1], beside),
    ]
    mine = wg.at[core, chan]
    weight_y = remote(mine, mine, w_s.at[0], w_r.at[0], ylo_peer)
    weight_x = [remote(mine, mine, w_s.at[d], w_r.at[d], x_peer(d)) for d in range(1, NX)]
    for copy in to_sibling + halos:
        copy.start()

    dimension_phases(core)
    for copy in loads[urgent:]:
        copy.wait()
    pltpu.make_async_copy(wout_in, wg.at[core, chan], weight_load).wait()
    for copy in [weight_y] + weight_x:
        copy.start()
    to_sibling[0].wait_recv()
    dimension_phases(1 - core)
    to_sibling[1].wait_recv()
    features = jnp.concatenate([ff[0], ff[1]], axis=1)

    def rs1_copy(w, i):
        device = (
            jnp.where(first, at(y, z + z_ahead(i), 0)[0], at(y + y_ahead(i), z, 1)[0]),
            chan,
        )
        slot = w * NZ + i
        return remote(ss.at[slot], rs1.at[slot], rs1_s.at[slot], rs1_r.at[slot], device)

    def forward(step, carry):
        w, i = step // NZ, lax.rem(step, NZ)
        nz = wave_number(step)
        cn, sn = trig[0, pl.ds(nz, 1), :], trig[1, pl.ds(nz, 1), :]
        for g in range(16):
            rows = slice(g * 16, (g + 1) * 16)
            ph[nz, rows, :] = (uv[0, rows, :] * cn + uv[1, rows, :] * sn).astype(BF16)
        total = dot(features, ph[nz], NT)
        ss[step] = total.astype(BF16)

        @pl.when(i < 7 - core)
        def _():
            rs1_copy(w, i).start()

        @pl.when(i >= 6)
        def _():
            own_sum[2 * w + i - 6] = total

        return carry

    lax.fori_loop(0, WAVES * NZ, forward, 0)

    weight_y.wait_recv()
    theirs = wg.at[core, (1 - ylo) * NX + x]
    weight_r = [
        remote(theirs, theirs, w_s.at[NX + d], w_r.at[NX + d], x_peer(d)) for d in range(1, NX)
    ]
    for copy in weight_r:
        copy.start()

    def make_sources():
        for copy in halos + to_sibling[2:]:
            copy.wait_recv()
        msg[...] = jnp.zeros((4, CD, 128), F32)
        rw_pad = jnp.concatenate([rw[...], jnp.zeros((NB, CD), F32)], axis=1)
        rw_t = jnp.transpose(rw_pad)[0:CD, :]
        for e in range(8):
            lanes = slice((e % 2) * 128, (e % 2 + 1) * 128)
            shift = -1.0 if e < 2 else (1.0 if e >= 6 else 0.0)
            rows = jnp.concatenate(
                [pc[2 * core + e // 2, :, lanes], jnp.zeros((5, 128), F32)], axis=0
            )
            at_x = lax.broadcasted_iota(jnp.int32, (8, 128), 0) == 0
            pt[e] = jnp.transpose(jnp.where(at_x, rows + shift, rows))
            block = fc[2 * core + e // 2, :, lanes].astype(F32)
            for m in range(NB):
                sc[e, :, m * 128 : (m + 1) * 128] = (block * rw_t[:, m : m + 1]).astype(BF16)

    def message(t, l):
        e = lists[t, l]
        used = jnp.where(l < counts[t], 1.0, 0.0).astype(F32)
        source = pt[e]
        lane = pl.ds(pl.multiple_of(lax.rem(t, 2) * 128, 128), 128)
        target = pc[1 + 2 * core + t // 2, :, lane]
        dx = (source[:, 0:1] - target[0:1, :]) * WIDTH
        dy = (source[:, 1:2] - target[1:2, :]) * CROSS
        dz = (source[:, 2:3] - target[2:3, :]) * CROSS
        r2 = dx * dx + dy * dy + dz * dz
        env = jnp.maximum(1.0 - r2 * (1.0 / (CUTOFF * CUTOFF)), 0.0)
        tt = jnp.minimum(jnp.sqrt(r2) * (1.0 / SPACING), float(NB - 1))
        value = jnp.exp(-tt * tt) * (env * env * used)
        ratio = jnp.exp(2.0 * tt)
        bas[0:128, :] = value.astype(BF16)
        for m in range(1, NB):
            value = value * (ratio * math.exp(-(2 * m - 1)))
            bas[m * 128 : (m + 1) * 128, :] = value.astype(BF16)
        return dot(sc[e], bas[...], NN)

    def messages(begin, end):
        def entry(k, carry):
            t = k // 4
            msg[t] += message(t, lax.rem(k, 4))
            return carry

        lax.fori_loop(begin, end, entry, 0)

    near = (FAR_Y, FAR_Z)
    far = (FAR_Z, FAR_Y)

    def near_device(d):
        return (jnp.where(first, at(y + d, z, 0)[0], at(y, z + d, 1)[0]), chan)

    def rs2_copy(w, d):
        unit = jnp.where(first, lax.rem(y + d, NY), lax.rem(z + d, NZ))
        slot = w * NZ + d
        return remote(
            t2.at[w, unit], rs2.at[slot], rs2_s.at[slot], rs2_r.at[slot], near_device(d)
        )

    def far_summed(w):
        for kind, here in kinds:

            @pl.when(here)
            def _():
                for i in range(NZ - 1 - kind):
                    rs1_copy(w, i).wait_recv()
                for h in range(1 + kind):
                    total = own_sum[2 * w + (h if kind else 1)]
                    for i in range(h, NZ - 1 - kind, 1 + kind):
                        total = total + rs1[w * NZ + i].astype(F32)
                    for u in range(4):
                        t2[w, 4 * h + u] = total[
                            32 * (u % 2) : 32 * (u % 2 + 1), 128 * (u // 2) : 128 * (u // 2 + 1)
                        ].astype(BF16)
                for d in near[kind]:
                    rs2_copy(w, d).start()

    def ag1_copy(w, d):
        unit = fg.at[own_nz[w], own_unit]
        slot = w * NZ + d
        return remote(unit, unit, ag1_s.at[slot], ag1_r.at[slot], near_device(d))

    def near_summed(w):
        for kind, here in kinds:

            @pl.when(here)
            def _():
                total = t2[w, z if kind else y].astype(F32)
                for d in near[kind]:
                    rs2_copy(w, d).wait_recv()
                    total = total + rs2[w * NZ + d].astype(F32)
                fg[own_nz[w], own_unit] = (flt[w] * (total * INVERSE)).astype(BF16)
                for d in near[kind]:
                    ag1_copy(w, d).start()

    def ag2_copy(kind, w, d):
        if kind == 0:
            group = fg.at[pl.ds(2 * z + w, 1)]
        else:
            group = fg.at[pl.ds(4 * y + 2 * w, 2)]
        slot = w * NZ + d
        device = (y_peer if kind else z_peer)(d)
        return remote(group, group, ag2_s.at[slot], ag2_r.at[slot], device)

    def near_gathered(w):
        for kind, here in kinds:

            @pl.when(here)
            def _():
                for d in near[kind]:
                    ag1_copy(w, d).wait_recv()
                for d in far[kind]:
                    ag2_copy(kind, w, d).start()

    def filtered(nz):
        top = jnp.concatenate([fg[nz, 0], fg[nz, 2]], axis=1)
        bottom = jnp.concatenate([fg[nz, 1], fg[nz, 3]], axis=1)
        return jnp.concatenate([top, bottom], axis=0)

    ewald_share = remote(ew.at[1 - core], ewr, ew_s, ew_r, sibling)

    def evaluate(w):
        for kind, here in kinds:

            @pl.when(here)
            def _():
                for i in range(4):
                    if kind == 0:
                        chunks = []
                        for d in ((0, 1), (7, 2), (6, 3), (5, 4))[i]:
                            if d:
                                ag2_copy(kind, w, d).wait_recv()
                            chunks.append(2 * lax.rem(z + NZ - d, NZ) + w)
                    else:
                        d = (0, 1, 3, 2)[i]
                        if d:
                            ag2_copy(kind, w, d).wait_recv()
                        base = 4 * lax.rem(y + NY - d, NY) + 2 * w
                        chunks = [base, base + 1]
                    sides = [filtered(nz) for nz in chunks]
                    if w == WAVES - 1 and i == 3:
                        for half in (1 - core, core):
                            lanes = pl.ds(pl.multiple_of(half * AD, AD), AD)
                            ew[half] += sum(
                                dot(a, ph[nz, :, lanes], NN) for a, nz in zip(sides, chunks)
                            )
                            if half is not core:
                                ewald_share.start()
                        continue
                    total = sum(dot(a, ph[nz], NN) for a, nz in zip(sides, chunks))
                    for half in range(2):
                        lanes = slice(half * AD, (half + 1) * AD)
                        if w == 0 and i == 0:
                            ew[half] = total[:, lanes]
                        else:
                            ew[half] += total[:, lanes]

    weights_on = remote(wg.at[core], wg.at[core], wf_s, wf_r, sibling)

    make_sources()
    far_summed(0)
    messages(0, 3)
    far_summed(1)
    messages(3, 6)
    near_summed(0)
    messages(6, 10)
    near_summed(1)
    messages(10, 13)
    near_gathered(0)
    messages(13, 16)
    near_gathered(1)
    evaluate(0)
    for copy in weight_x + weight_r:
        copy.wait_recv()
    weights_on.start()
    evaluate(1)

    ewald_share.wait_recv()
    for t in range(4):
        lanes = slice(t * 128, (t + 1) * 128)
        pair_lanes = slice((t % 2) * 128, (t % 2 + 1) * 128)
        ewald = (ew[core, :, lanes] + ewr[:, lanes]) * INVERSE
        mixed = (
            fc[1 + 2 * core + t // 2, :, pair_lanes].astype(F32) + msg[t] + ewald
        ).astype(BF16)
        ms[2 * t] = mixed[:, 0:64]
        ms[2 * t + 1] = mixed[:, 64:128]
    exchange = []
    for i, (dy, dx) in enumerate(FAR_CHAN):
        device = (brick, lax.rem(ylo + dy, 2) * NX + lax.rem(x + dx, NX))
        exchange.append(
            remote(ms.at[device[1]], mr.at[chan], a2a_s.at[i], a2a_r.at[i], device)
        )
        exchange[-1].start()
    mr[chan] = ms[chan]
    remote(wg.at[1 - core], wg.at[1 - core], wf_s, wf_r, sibling).wait_recv()
    for copy in exchange:
        copy.wait_recv()

    eye = (
        lax.broadcasted_iota(jnp.int32, (64, 64), 0)
        == lax.broadcasted_iota(jnp.int32, (64, 64), 1)
    ).astype(BF16)
    values = dot(eye, mr[...].reshape(C, 64), NT)
    mean_square = jnp.sum(values * values, axis=1, keepdims=True) * (1.0 / C)
    normed = (values * lax.rsqrt(mean_square + EPS) * gain[...]).astype(BF16)
    hidden = dot(normed, wg[0].reshape(C, HID), NN)
    active = jax.nn.gelu(hidden).astype(BF16)
    out[...] = (values + dot(active, wg[1].reshape(C, HID), NT)).astype(BF16)

    for copy in to_sibling + halos + weight_x + weight_r + [weight_y, weights_on, ewald_share]:
        copy.wait_send()
    for copy in exchange:
        copy.wait_send()
    for kind, here in kinds:

        @pl.when(here)
        def _():
            for w in range(WAVES):
                for i in range(NZ - 1 - kind):
                    rs1_copy(w, i).wait_send()
                for d in near[kind]:
                    rs2_copy(w, d).wait_send()
                    ag1_copy(w, d).wait_send()
                for d in far[kind]:
                    ag2_copy(kind, w, d).wait_send()


def body(features, positions, lists, counts, fourier_filter, radial_weights, norm_gain, mlp_in, mlp_out):
    dma = pltpu.SemaphoreType.DMA
    slots = WAVES * NZ
    scratch = [
        pltpu.VMEM((6, CD, 256), BF16),
        pltpu.VMEM((6, 3, 256), F32),
        pltpu.SMEM((4, 4), jnp.int32),
        pltpu.SMEM((4,), jnp.int32),
        pltpu.VMEM((NB, CD), F32),
        pltpu.VMEM((1, C), F32),
        pltpu.VMEM((KS, 256, 2 * AD), BF16),
        pltpu.VMEM((2, KS, 2 * AD), F32),
        pltpu.VMEM((2, 256, 2 * AD), F32),
        pltpu.VMEM((2, CD, AD), BF16),
        pltpu.VMEM((slots, CD, 256), BF16),
        pltpu.VMEM((2 * WAVES, CD, 256), F32),
        pltpu.VMEM((slots, CD, 256), BF16),
        pltpu.VMEM((WAVES, NZ, 32, 128), BF16),
        pltpu.VMEM((slots, 32, 128), BF16),
        pltpu.VMEM((KS, 4, 32, 128), BF16),
        pltpu.VMEM((WAVES, 32, 128), F32),
        pltpu.VMEM((8, 128, 8), F32),
        pltpu.VMEM((8, CD, NB * 128), BF16),
        pltpu.VMEM((NB * 128, 128), BF16),
        pltpu.VMEM((4, CD, 128), F32),
        pltpu.VMEM((2, CD, AD), F32),
        pltpu.VMEM((CD, AD), F32),
        pltpu.VMEM((2, NCHAN, CD, HID), BF16),
        pltpu.VMEM((NCHAN, CD, 64), BF16),
        pltpu.VMEM((NCHAN, CD, 64), BF16),
        dma((13,)),
        dma((3,)), dma((3,)),
        dma((2,)), dma((2,)),
        dma((slots,)), dma((slots,)),
        dma((slots,)), dma((slots,)),
        dma((slots,)), dma((slots,)),
        dma((slots,)), dma((slots,)),
        dma, dma,
        dma((2 * NX,)), dma((2 * NX,)),
        dma, dma,
        dma((NCHAN,)), dma((NCHAN,)),
    ]
    return pl.pallas_call(
        kernel,
        out_shape=jax.ShapeDtypeStruct((64, C), BF16),
        in_specs=[pl.BlockSpec(memory_space=pltpu.HBM)] * 9,
        out_specs=pl.BlockSpec(memory_space=pltpu.VMEM),
        scratch_shapes=scratch,
        compiler_params=pltpu.CompilerParams(
            collective_id=0, has_side_effects=True, vmem_limit_bytes=60 * 2**20
        ),
    )(
        features, positions, lists, counts, fourier_filter, radial_weights,
        norm_gain.reshape(1, C), mlp_in.T, mlp_out,
    ).T


def solution(mesh):
    return jax.shard_map(
        body,
        mesh=mesh,
        in_specs=(
            P("chan", "brick"),
            P(None, "brick"),
            P("brick", None),
            P("brick"),
            P("chan", None),
            P(None, "chan"),
            P(),
            P(None, "chan"),
            P("chan", None),
        ),
        out_specs=P(None, ("brick", "chan")),
        check_vma=False,
    )
```
